128 devices in a mesh: row: 4 (over z), col: 4 (over y_lo, core), depth: 8 (over y_hi, x).
Axes of the slice: x: 4, y: 4 (y_hi: 2, y_lo: 2; y = y_hi * 2 + y_lo), z: 4, core: 2. Of those that a mesh axis runs over, the one named last changes fastest.
Arguments:
- inputs: bfloat16 [8, 512, 8192], P('depth', 'row', 'col'), may hold values from -13 to 13
- w_query: bfloat16 [8192, 4096], P('col', 'row'), may hold values from -0.06629126 to 0.06629126
- w_key: bfloat16 [8192, 512], P('col', 'row'), may hold values from -0.06629126 to 0.06629126
- w_value: bfloat16 [8192, 512], P('col', 'row'), may hold values from -0.0625 to 0.0625
- w_output: bfloat16 [4096, 8192], P('row', 'col'), may hold values from -0.09375 to 0.09375
- segment_ids: int32 [8, 512], P('depth'), may hold values from 0 to 2, never falling along the last dimension, each value on 1 to 256 neighbouring positions
- position_gaps: int32 [8, 512], P('depth'), may hold values from 1 to 4
- cotangent: bfloat16 [8, 512, 8192], P('depth', 'row', 'col'), may hold values from -6 to 6
Outputs:
- attn_out: bfloat16 [8, 512, 8192], P('depth', 'row', 'col')
- grad_inputs: bfloat16 [8, 512, 8192], P('depth', 'row', 'col')
- grad_wq: float32 [8192, 4096], P(('col', 'depth'), 'row')
- grad_wk: float32 [8192, 512], P(('col', 'depth'), 'row')
- grad_wv: float32 [8192, 512], P(('col', 'depth'), 'row')
- grad_wo: float32 [4096, 8192], P(('row', 'depth'), 'col')
The draws below stay inside these ranges and needn't reach their ends.
Inputs may be any that keep to these rules, and one draw needn't show every extreme that they name: `segment_ids`: within each pack the ids never fall; each of the 3 documents has 1 to 256 tokens, and one has exactly 256.
All inputs are finite; a program needn't handle non-finite values.
Results may differ from the reference program's by a relative error of at most 0.0152.
Values may be sent and summed in bfloat16 or wider, within the bound.
No kernel may reach another device: no remote copies, remote signals or barrier semaphores. Data moves between devices by JAX's collectives and lax.ppermute only.
A program may use at most 128 MiB of HBM per device.

```python
import math
import jax
import jax.numpy as jnp
import numpy as np
from jax import lax

MODEL_WIDTH = 8192
QUERY_HEADS = 32
KEY_VALUE_HEADS = 4
HEAD_SIZE = 128
SEQS = 3
PACK_TOKENS = 512
GROUPS = 8
MOST = 256
QUERY_FEATURES = 4096
FKV = 512


def shared_key_weight(key):
    return jnp.clip(jax.random.normal(key, (MODEL_WIDTH, FKV), jnp.float32), -6.0, 6.0) * MODEL_WIDTH ** (-0.5)


def draw_w_key(key, part):
    return shared_key_weight(key).astype(jnp.bfloat16)


def draw_w_query(key, part):
    key = jax.random.fold_in(key, 7)
    fresh = jnp.clip(jax.random.normal(key, (MODEL_WIDTH, QUERY_FEATURES), jnp.float32), -6.0, 6.0) * MODEL_WIDTH ** (-0.5)
    return fresh.astype(jnp.bfloat16)


def draw_inputs(key, part):
    key = jax.random.fold_in(key, 3)
    subkeys = jax.random.split(key, 1)
    return jnp.clip(jax.random.normal(subkeys[0], (GROUPS, PACK_TOKENS, MODEL_WIDTH), jnp.float32), -4.0, 4.0).astype(jnp.bfloat16)


def touch_ends(values, key, smallest, high):
    longest = values.shape.index(max(values.shape))
    spots = []
    for shift in (0, 1):
        where = [jax.random.randint(jax.random.fold_in(key, axis), (), 0, length) for axis, length in enumerate(values.shape)]
        where[longest] = (where[longest] + shift) % values.shape[longest]
        spots.append(tuple(where))
    return values.at[spots[0]].set(smallest).at[spots[1]].set(high)


def shard_levels(rng, dims, cuts, low, largest):
    loudness = 1.0
    for dim, blocks in cuts:
        heights = jax.random.uniform(jax.random.fold_in(jax.random.fold_in(rng, 6), dim), (blocks,), jnp.float32, low / len(cuts), largest / len(cuts))
        loudness = loudness * jnp.repeat(jnp.exp(heights), dims[dim] // blocks).reshape((-1,) + (1,) * (len(dims) - 1 - dim))
    return loudness


def split_up(count, total, bound, lean):
    loads = [(1 << 20) // math.isqrt(standing ** lean) + 1 for standing in range(2, count + 1)]
    surplus, holding = total - bound - (count - 1), [1] * (count - 1)
    while surplus > 0:
        movable = [i for i in range(count - 1) if holding[i] < bound]
        whole, remaining = sum([loads[i] for i in movable]), surplus
        for i in movable:
            addition = min(bound - holding[i], max(1, remaining * loads[i] // whole), surplus)
            holding[i] = holding[i] + addition
            surplus = surplus - addition
    return np.array([bound] + holding)


def ragged_sizes(own_key, number_of, total, limit, lean):
    if number_of == 2:
        one = jax.random.randint(own_key, (), max(1, total - limit), min(limit, total - 1) + 1)
        return jnp.stack([one, total - one])
    lengths = jnp.asarray(split_up(number_of, total, limit, lean), jnp.int32)
    pairs = (number_of - 1) // 2
    giver, taker = lengths[1:1 + 2 * pairs:2], lengths[2:2 + 2 * pairs:2]
    margin = jnp.minimum(giver - 1, limit - taker)
    shifted = jax.random.randint(jax.random.fold_in(own_key, 1), (pairs,), 0, 1 << 20) % (margin + 1)
    lengths = lengths.at[1:1 + 2 * pairs:2].set(giver - shifted).at[2:2 + 2 * pairs:2].set(taker + shifted)
    return lengths[jax.random.permutation(jax.random.fold_in(own_key, 2), number_of)]


def centred(stream_key, extent, spread, reach, shards=(), held_as=jnp.bfloat16):
    loudness = shard_levels(stream_key, extent, shards, -0.22, 0.18) if shards else 1.0
    result = jax.random.normal(stream_key, extent, jnp.float32) * spread * loudness
    return jnp.minimum(jnp.maximum(result, -reach), reach).astype(held_as)


def setup_inputs(seed: int = 0) -> dict:
    arg_keys = jax.random.split(jax.random.key(seed), 9)
    return {
        "inputs": draw_inputs(jax.random.fold_in(arg_keys[8], 71), 0),
        "w_query": draw_w_query(jax.random.fold_in(arg_keys[8], 71), 0),
        "w_key": draw_w_key(jax.random.fold_in(arg_keys[8], 71), 0),
        "w_value": centred(arg_keys[3], (MODEL_WIDTH, FKV), MODEL_WIDTH ** -0.5, 0.0625, ((0, 4), (1, 4))),
        "w_output": centred(arg_keys[4], (QUERY_FEATURES, MODEL_WIDTH), QUERY_FEATURES ** -0.5, 0.09375, ((0, 4), (1, 4))),
        "segment_ids": jax.vmap(lambda own: jnp.searchsorted(jnp.cumsum(ragged_sizes(own, SEQS, PACK_TOKENS, MOST, 1)), jnp.arange(PACK_TOKENS), side="right"))(jax.random.split(arg_keys[5], GROUPS)).reshape((GROUPS, PACK_TOKENS)).astype(jnp.int32),
        "position_gaps": touch_ends(jax.random.randint(arg_keys[6], (GROUPS, PACK_TOKENS), 1, 5), jax.random.fold_in(arg_keys[6], 1), 1, 4).astype(jnp.int32),
        "cotangent": centred(arg_keys[7], (GROUPS, PACK_TOKENS, MODEL_WIDTH), 1.0, 6.0, ((0, 8), (1, 4), (2, 4))),
    }


def tables(positions):
    frequency = 1.0 / 10000.0 ** (jnp.arange(HEAD_SIZE // 2, dtype=jnp.float32) * (2.0 / HEAD_SIZE))
    angles = positions[:, None] * frequency[None, :]
    return (jnp.cos(angles), jnp.sin(angles))

def apply_rotary(vectors, cosine_lookup, sine_lookup):
    half_width = vectors.shape[-1] // 2
    first_half = vectors[..., :half_width]
    second_half = vectors[..., half_width:]
    cos_part = cosine_lookup[:, None, :]
    sin_part = sine_lookup[:, None, :]
    return jnp.concatenate([first_half * cos_part - second_half * sin_part, second_half * cos_part + first_half * sin_part], axis=-1)

def rounded_values(value_rows):
    return lax.optimization_barrier(value_rows.astype(jnp.bfloat16)).astype(jnp.float32)

def reference(inputs, w_query, w_key, w_value, w_output, segment_ids, position_gaps, cotangent):
    per_key_value = QUERY_HEADS // KEY_VALUE_HEADS
    score_scale = 1.0 / math.sqrt(HEAD_SIZE)
    token_position = jnp.arange(PACK_TOKENS, dtype=jnp.int32)
    weights_all = jnp.concatenate([w_query, w_key, w_value], axis=1)

    def one_pack(sums_so_far, slices):
        grad_w, grad_out = sums_so_far
        pack_inputs, segments, gaps, pack_cotangent = slices
        same_seq = segments[:, None] == segments[None, :]
        earlier = (same_seq & (token_position[None, :] < token_position[:, None])).astype(jnp.float32)
        positions = jnp.dot(earlier, gaps.astype(jnp.float32), precision=lax.Precision.HIGHEST)
        allowed = same_seq & (token_position[None, :] <= token_position[:, None])
        cosine_lookup, sine_lookup = tables(positions)
        q_raw = jnp.dot(pack_inputs, w_query, preferred_element_type=jnp.float32)
        key_unrotated = jnp.dot(pack_inputs, w_key, preferred_element_type=jnp.float32)
        value_unrotated = jnp.dot(pack_inputs, w_value, preferred_element_type=jnp.float32)
        query_rows = rounded_values(apply_rotary(q_raw.reshape(PACK_TOKENS, QUERY_HEADS, HEAD_SIZE), cosine_lookup, sine_lookup))
        key_rows = rounded_values(apply_rotary(key_unrotated.reshape(PACK_TOKENS, KEY_VALUE_HEADS, HEAD_SIZE), cosine_lookup, sine_lookup))
        value_rows = rounded_values(value_unrotated).reshape(PACK_TOKENS, KEY_VALUE_HEADS, HEAD_SIZE)
        query_quad = query_rows.reshape(PACK_TOKENS, KEY_VALUE_HEADS, per_key_value, HEAD_SIZE)
        scores = jnp.einsum('tkgd,skd->kgts', query_quad, key_rows) * score_scale
        masked = jnp.where(allowed[None, None], scores, -jnp.inf)
        row_max = lax.optimization_barrier(jnp.max(masked, axis=-1, keepdims=True))
        unnormed = jnp.exp(masked - row_max)
        probability = unnormed / lax.optimization_barrier(jnp.sum(unnormed, axis=-1, keepdims=True))
        probability_b = rounded_values(probability)
        mixed = jnp.einsum('kgts,skd->tkgd', probability_b, value_rows).reshape(PACK_TOKENS, QUERY_FEATURES).astype(jnp.bfloat16)
        attn_out = jnp.dot(mixed, w_output, preferred_element_type=jnp.float32).astype(jnp.bfloat16)
        gradient_blend = jnp.dot(pack_cotangent, w_output.T, preferred_element_type=jnp.float32).astype(jnp.bfloat16)
        gradient_quad = gradient_blend.astype(jnp.float32).reshape(PACK_TOKENS, KEY_VALUE_HEADS, per_key_value, HEAD_SIZE)
        grad_probs = jnp.einsum('tkgd,skd->kgts', gradient_quad, value_rows)
        row_dot = lax.optimization_barrier(jnp.sum(probability * grad_probs, axis=-1, keepdims=True))
        grad_scores = rounded_values(probability * (grad_probs - row_dot) * score_scale)
        grad_q_rot = jnp.einsum('kgts,skd->tkgd', grad_scores, key_rows).reshape(PACK_TOKENS, QUERY_HEADS, HEAD_SIZE)
        grad_k_rot = jnp.einsum('kgts,tkgd->skd', grad_scores, query_quad)
        grad_v = jnp.einsum('kgts,tkgd->skd', probability_b, gradient_quad)
        grad_q = apply_rotary(grad_q_rot, cosine_lookup, -sine_lookup).reshape(PACK_TOKENS, QUERY_FEATURES)
        grad_k = apply_rotary(grad_k_rot, cosine_lookup, -sine_lookup).reshape(PACK_TOKENS, FKV)
        grad_qkv = jnp.concatenate([grad_q, grad_k, grad_v.reshape(PACK_TOKENS, FKV)], axis=1).astype(jnp.bfloat16)
        grad_inputs = jnp.dot(grad_qkv, weights_all.T, preferred_element_type=jnp.float32).astype(jnp.bfloat16)
        grad_w = grad_w + jnp.dot(pack_inputs.T, grad_qkv, preferred_element_type=jnp.float32)
        grad_out = grad_out + jnp.dot(mixed.T, pack_cotangent, preferred_element_type=jnp.float32)
        return ((grad_w, grad_out), (attn_out, grad_inputs))
    start_sums = (jnp.zeros((MODEL_WIDTH, QUERY_FEATURES + 2 * FKV), jnp.float32), jnp.zeros((QUERY_FEATURES, MODEL_WIDTH), jnp.float32))
    (grad_w, grad_out), (attn_out, grad_inputs) = lax.scan(one_pack, start_sums, (inputs, segment_ids, position_gaps, cotangent))
    return (attn_out, grad_inputs, grad_w[:, :QUERY_FEATURES], grad_w[:, QUERY_FEATURES:QUERY_FEATURES + FKV], grad_w[:, QUERY_FEATURES + FKV:], grad_out)
```

```python
import math

import jax
import jax.numpy as jnp
from jax import lax
from jax.sharding import PartitionSpec as P

HEAD = 128
OFFSETS = (0, 3, 1, 2)
BF = jnp.bfloat16
F32 = jnp.float32


def shift_row(v, s):
    return lax.ppermute(v, "row", [(i, (i + s) % 4) for i in range(4)])


def shift_x(v, s):
    return lax.ppermute(
        v, "depth", [(h * 4 + i, h * 4 + (i + s) % 4) for h in range(2) for i in range(4)]
    )


def swap_core(v):
    return lax.ppermute(v, "col", [(i, i ^ 1) for i in range(4)])


def swap_ylo(v):
    return lax.ppermute(v, "col", [(i, i ^ 2) for i in range(4)])


def swap_yhi(v):
    return lax.ppermute(v, "depth", [(i, i ^ 4) for i in range(8)])


def swap_other(v):
    pairs = [(c * 8 + d, (c ^ 2) * 8 + (d ^ 4)) for c in range(4) for d in range(8)]
    return lax.ppermute(v, ("col", "depth"), pairs)


def mm(a, b):
    return jnp.dot(a, b, preferred_element_type=F32)


def mm_nt(a, b):
    return lax.dot_general(a, b, (((1,), (1,)), ((), ())), preferred_element_type=F32)


def mm_tn(a, b):
    return lax.dot_general(a, b, (((0,), (0,)), ((), ())), preferred_element_type=F32)


def after(v, *deps):
    return lax.optimization_barrier((v,) + deps)[0]


def gather_row(v):
    half = v.shape[0] // 2
    left = shift_row(v, 1)
    right = shift_row(v, -1)
    first = shift_row(left[:half], 1)
    second = shift_row(right[half:], -1)
    return jnp.concatenate([v, left, right, first, second], axis=0), first


def ring_sum(parts, shift):
    opp = parts(3).astype(BF)
    half = opp.shape[0] // 2
    from_left = shift(opp[:half], 1)
    from_right = shift(opp[half:], -1)
    right = parts(2)
    right = jnp.concatenate([right[:half] + from_left.astype(F32), right[half:]], axis=0)
    left = parts(1)
    left = jnp.concatenate([left[:half], left[half:] + from_right.astype(F32)], axis=0)
    got_left = shift(right.astype(BF), 1)
    got_right = shift(left.astype(BF), -1)
    return parts(0) + got_left.astype(F32) + got_right.astype(F32)


def sum_col(part, core, ylo):
    n = part.shape[1]
    blocks = part.reshape(2, 2, 128, n)
    send = lax.dynamic_index_in_dim(blocks, 1 - core, 1, keepdims=False).astype(BF)
    keep = lax.dynamic_index_in_dim(blocks, core, 1, keepdims=False)
    both = keep + swap_core(send).astype(F32)
    send = lax.dynamic_index_in_dim(both, 1 - ylo, 0, keepdims=False).astype(BF)
    keep = lax.dynamic_index_in_dim(both, ylo, 0, keepdims=False)
    return keep + swap_ylo(send).astype(F32)


def all_sum_col(part):
    part = part + swap_core(part.astype(BF)).astype(F32)
    return part + swap_ylo(part.astype(BF)).astype(F32)


def order_ylo(mine, other, ylo):
    first = jnp.where(ylo == 0, mine, other)
    second = jnp.where(ylo == 0, other, mine)
    return jnp.stack([first, second])


def order_core(mine, other, core):
    n = mine.shape[-1]
    first = jnp.where(core == 0, mine, other)
    second = jnp.where(core == 0, other, mine)
    return jnp.stack([first, second], axis=1).reshape(512, n)


def rotate(v, cos, sin):
    t = v.shape[0]
    w = v.reshape(t, -1, 2, 64)
    a, b = w[:, :, 0], w[:, :, 1]
    c, s = cos[:, None], sin[:, None]
    return jnp.stack([a * c - b * s, b * c + a * s], axis=2).reshape(v.shape)


def on_device(inputs, w_query, w_key, w_value, w_output, segment_ids, position_gaps, cotangent):
    scale = 1.0 / math.sqrt(HEAD)
    row = lax.axis_index("row")
    col = lax.axis_index("col")
    depth = lax.axis_index("depth")
    core, ylo = col % 2, col // 2
    yhi, xx = depth // 4, depth % 4
    x_own, dy_own = inputs[0], cotangent[0]
    half_feat = x_own.shape[1] // 2

    def half(v, which):
        return lax.dynamic_slice_in_dim(v, which * half_feat, half_feat, 1)

    x_other_own = swap_yhi(half(x_own, 1 - yhi))
    dy_other_own = swap_yhi(half(dy_own, 1 - yhi))

    offsets = jnp.array(OFFSETS, jnp.int32)
    token = (((row + offsets) % 4)[:, None] * 128 + jnp.arange(128, dtype=jnp.int32)).reshape(512)
    segments = segment_ids[0]
    gaps = position_gaps[0].astype(F32)
    seg_rel = jnp.take(segments.reshape(4, 128), (row + offsets) % 4, axis=0).reshape(512)
    natural = jnp.arange(512, dtype=jnp.int32)
    earlier = (seg_rel[:, None] == segments[None, :]) & (natural[None, :] < token[:, None])
    positions = jnp.sum(jnp.where(earlier, gaps[None, :], 0.0), axis=1)
    frequency = 1.0 / 10000.0 ** (jnp.arange(64, dtype=F32) * (2.0 / HEAD))
    angles = positions[:, None] * frequency[None, :]
    cos_all, sin_all = jnp.cos(angles), jnp.sin(angles)

    def own(v):
        return lax.dynamic_slice_in_dim(v, col * 128, 128, 0)

    cos_own, sin_own = own(cos_all), own(sin_all)
    seg_own, token_own = own(seg_rel), own(token)
    allowed = (seg_own[:, None] == seg_rel[None, :]) & (token[None, :] <= token_own[:, None])

    x_all, x_done = gather_row(x_own)
    dy_all, dy_done = gather_row(after(dy_own, x_done))
    dy_other, dyo_done = gather_row(after(dy_other_own, dy_done))
    x_other, _ = gather_row(after(x_other_own, dyo_done))

    kv = all_sum_col(jnp.concatenate([mm(x_all, w_key), mm(x_all, w_value)], axis=1))
    keys = rotate(kv[:, :128], cos_all, sin_all).astype(BF)
    values = kv[:, 128:].astype(BF)
    q_raw = sum_col(mm(x_all, w_query), core, ylo)
    queries = rotate(q_raw, cos_own, sin_own).astype(BF)

    q8 = queries.reshape(128, 8, 128)
    scores = jnp.einsum("thd,sd->hts", q8, keys, preferred_element_type=F32) * scale
    masked = jnp.where(allowed[None], scores, -jnp.inf)
    unnormed = jnp.exp(masked - jnp.max(masked, axis=-1, keepdims=True))
    prob = unnormed / jnp.sum(unnormed, axis=-1, keepdims=True)
    prob_b = prob.astype(BF)
    mixed_own = jnp.einsum("hts,sd->thd", prob_b, values, preferred_element_type=F32)
    mixed_own = mixed_own.astype(BF).reshape(128, 1024)

    def gather_y(v):
        h = v.shape[0] // 2
        a = swap_ylo(v)
        b = swap_other(v)
        mine = order_ylo(v, a, ylo)
        pack = order_core(mine, swap_core(mine), core)
        opp = jnp.concatenate([swap_other(a[:h]), swap_ylo(b[h:])], axis=0)
        theirs = order_ylo(opp, b, ylo)
        other = order_core(theirs, swap_core(theirs), core)
        return pack, other

    mixed, mixed_other = gather_y(mixed_own)

    grad_mixed = sum_col(mm_nt(dy_all, w_output), core, ylo).astype(BF)

    attn_out = ring_sum(lambda j: mm(mixed[j * 128 : j * 128 + 128], w_output), shift_row)

    dy_half = half(dy_all, yhi)

    def wo_part(j):
        at = (xx + OFFSETS[j]) % 4 * 128

        def heads(m):
            return jnp.concatenate(
                [
                    lax.dynamic_slice_in_dim(m, at, 128, 1),
                    lax.dynamic_slice_in_dim(m, at + 512, 128, 1),
                ],
                axis=1,
            )

        return mm_tn(heads(mixed), dy_half) + mm_tn(heads(mixed_other), dy_other)

    wo_sum = ring_sum(wo_part, shift_x)
    wo_keep = lax.dynamic_slice_in_dim(wo_sum, yhi * 128, 128, 0)
    wo_send = lax.dynamic_slice_in_dim(wo_sum, (1 - yhi) * 128, 128, 0).astype(BF)
    wo_got = swap_yhi(wo_send).astype(F32)
    grad_wo = jnp.where(
        yhi == 0,
        jnp.concatenate([wo_keep, wo_got], axis=1),
        jnp.concatenate([wo_got, wo_keep], axis=1),
    )

    g8 = grad_mixed.reshape(128, 8, 128)
    grad_probs = jnp.einsum("thd,sd->hts", g8, values, preferred_element_type=F32)
    row_dot = jnp.sum(prob * grad_probs, axis=-1, keepdims=True)
    grad_scores = (prob * (grad_probs - row_dot) * scale).astype(BF)
    dq_rot = jnp.einsum("hts,sd->thd", grad_scores, keys, preferred_element_type=F32)
    dk_part = jnp.einsum("hts,thd->sd", grad_scores, q8, preferred_element_type=F32)
    dv_part = jnp.einsum("hts,thd->sd", prob_b, g8, preferred_element_type=F32)
    dq_own = rotate(dq_rot.reshape(128, 1024), cos_own, -sin_own).astype(BF)
    dkv = all_sum_col(jnp.concatenate([dk_part, dv_part], axis=1))
    dk = rotate(dkv[:, :128], cos_all, -sin_all).astype(BF)
    dkv = jnp.concatenate([dk, dkv[:, 128:].astype(BF)], axis=1)
    dkv_other = swap_yhi(dkv)
    dq, dq_other = gather_y(dq_own)
    grad = jnp.concatenate([dq, dkv], axis=1)
    grad_other = jnp.concatenate([dq_other, dkv_other], axis=1)
    weights = jnp.concatenate([w_query, w_key, w_value], axis=1)

    grad_inputs = ring_sum(lambda j: mm_nt(grad[j * 128 : j * 128 + 128], weights), shift_row)

    x_half = half(x_all, yhi)

    def w_part(j):
        at = (xx + OFFSETS[j]) % 4 * 256
        return mm_tn(lax.dynamic_slice_in_dim(x_half, at, 256, 1), grad) + mm_tn(
            lax.dynamic_slice_in_dim(x_other, at, 256, 1), grad_other
        )

    grad_w = ring_sum(w_part, shift_x)
    return (
        attn_out.astype(BF)[None],
        grad_inputs.astype(BF)[None],
        grad_w[:, :1024],
        grad_w[:, 1024:1152],
        grad_w[:, 1152:],
        grad_wo,
    )


def solution(mesh):
    return jax.shard_map(
        on_device,
        mesh=mesh,
        in_specs=(
            P("depth", "row", "col"),
            P("col", "row"),
            P("col", "row"),
            P("col", "row"),
            P("row", "col"),
            P("depth", None),
            P("depth", None),
            P("depth", "row", "col"),
        ),
        out_specs=(
            P("depth", "row", "col"),
            P("depth", "row", "col"),
            P(("col", "depth"), "row"),
            P(("col", "depth"), "row"),
            P(("col", "depth"), "row"),
            P(("row", "depth"), "col"),
        ),
        check_vma=False,
    )
```

```python
import math

import jax
import jax.numpy as jnp
from jax import lax
from jax.experimental import pallas as pl
from jax.experimental.pallas import tpu as pltpu
from jax.sharding import PartitionSpec as P

HEAD = 128
OFFSETS = (0, 3, 1, 2)
BF = jnp.bfloat16
F32 = jnp.float32
SCALE = 1.0 / math.sqrt(HEAD)
MIB = 1 << 20


def shift_row(v, s):
    return lax.ppermute(v, "row", [(i, (i + s) % 4) for i in range(4)])


def shift_x(v, s):
    return lax.ppermute(
        v, "depth", [(h * 4 + i, h * 4 + (i + s) % 4) for h in range(2) for i in range(4)]
    )


def swap_core(v):
    return lax.ppermute(v, "col", [(i, i ^ 1) for i in range(4)])


def swap_ylo(v):
    return lax.ppermute(v, "col", [(i, i ^ 2) for i in range(4)])


def swap_yhi(v):
    return lax.ppermute(v, "depth", [(i, i ^ 4) for i in range(8)])


def swap_other(v):
    pairs = [(c * 8 + d, (c ^ 2) * 8 + (d ^ 4)) for c in range(4) for d in range(8)]
    return lax.ppermute(v, ("col", "depth"), pairs)


def after(v, *deps):
    return lax.optimization_barrier((v,) + deps)[0]


def gather_row(v):
    half = v.shape[0] // 2
    left = shift_row(v, 1)
    right = shift_row(v, -1)
    first = shift_row(left[:half], 1)
    second = shift_row(right[half:], -1)
    return [v, left, right, first, second]


def rows_at(block, size=128):
    return pl.ds(pl.multiple_of(block * size, size), size)


def fill_row_pieces(ref, pieces, place, base=0):
    own, left, right, first, second = pieces
    ref[rows_at(base + place(0)), :] = own
    ref[rows_at(base + place(1)), :] = left
    ref[rows_at(base + place(2)), :] = right
    opp = (base + place(3)) * 2
    ref[rows_at(opp, 64), :] = first
    ref[rows_at(opp + 1, 64), :] = second


def dot(a, b):
    return jnp.dot(a, b, preferred_element_type=F32)


def dot_nt(a, b):
    return lax.dot_general(a, b, (((1,), (1,)), ((), ())), preferred_element_type=F32)


def dot_tn(a, b):
    return lax.dot_general(a, b, (((0,), (0,)), ((), ())), preferred_element_type=F32)


def rotate(v, cos, sin):
    return v * cos + pltpu.roll(v, 64, 1) * sin


def whole(shape):
    return pl.BlockSpec(shape, lambda *_: (0,) * len(shape))


def sds(shape, dtype=BF):
    return jax.ShapeDtypeStruct(shape, dtype)


def call(body, scal, args, in_specs, outs, out_specs, grid=(1,), scratch=(), flops=0, limit=24):
    moved = sum(a.size * a.dtype.itemsize for a in args)
    return pl.pallas_call(
        body,
        grid_spec=pltpu.PrefetchScalarGridSpec(
            num_scalar_prefetch=1,
            grid=grid,
            in_specs=in_specs,
            out_specs=out_specs,
            scratch_shapes=list(scratch),
        ),
        out_shape=outs,
        compiler_params=pltpu.CompilerParams(vmem_limit_bytes=limit * MIB),
        cost_estimate=pl.CostEstimate(flops=flops, bytes_accessed=moved, transcendentals=0),
    )(scal, *args)


def qkv_body(s, xo, xl, xr, xf, xs2, wq, wk, wv, kv, send, keep, xs):
    i = pl.program_id(0)
    c = s[0]

    @pl.when(i == 0)
    def _():
        pieces = [r[...] for r in (xo, xl, xr, xf, xs2)]
        fill_row_pieces(xs, pieces, lambda j: 3 ^ c ^ j)
        kv[:, :128] = dot(xs[...], wk[...]).astype(BF)
        kv[:, 128:] = dot(xs[...], wv[...]).astype(BF)

    @pl.when(i > 0)
    def _():
        r = dot(xs[...], wq[...]).astype(BF)
        store_pair(r, send, keep)


def qkv_parts(scal, x, wq, wk, wv):
    feat, nq = wq.shape
    tile = 256
    col = lambda i, *_: (0, jnp.maximum(i - 1, 0))
    return call(
        qkv_body,
        scal,
        [*x, wq, wk, wv],
        [whole(p.shape) for p in x]
        + [pl.BlockSpec((feat, tile), col), whole(wk.shape), whole(wv.shape)],
        [sds((512, 256)), sds((256, nq)), sds((256, nq))],
        [whole((512, 256)), pl.BlockSpec((256, tile), col), pl.BlockSpec((256, tile), col)],
        grid=(1 + nq // tile,),
        scratch=[pltpu.VMEM((512, feat), BF)],
        flops=2 * 512 * feat * (nq + 256),
    )


def store_pair(r, send, keep):
    send[:128] = r[:128]
    send[128:] = r[256:384]
    keep[:128] = r[128:256]
    keep[128:] = r[384:]


def gm_body(s, xo, xl, xr, xf, xs2, wo, send, keep, xs):
    c = s[0]

    @pl.when(pl.program_id(0) == 0)
    def _():
        pieces = [r[...] for r in (xo, xl, xr, xf, xs2)]
        fill_row_pieces(xs, pieces, lambda j: 3 ^ c ^ j)

    r = dot_nt(xs[...], wo[...]).astype(BF)
    store_pair(r, send, keep)


def gm_parts(scal, dy, wo):
    nq, feat = wo.shape
    tile = 256
    return call(
        gm_body,
        scal,
        [*dy, wo],
        [whole(p.shape) for p in dy] + [pl.BlockSpec((tile, feat), lambda i, *_: (i, 0))],
        [sds((256, nq)), sds((256, nq))],
        [pl.BlockSpec((256, tile), lambda i, *_: (0, i))] * 2,
        grid=(nq // tile,),
        scratch=[pltpu.VMEM((512, feat), BF)],
        flops=2 * 512 * feat * nq,
    )


def add_pair_body(s, keep, got, send, left):
    t = keep[...].astype(F32) + got[...].astype(F32)
    send[...] = t[:128].astype(BF)
    left[...] = t[128:].astype(BF)


def add_pair(scal, keep, got):
    n = keep.shape[1]
    return call(
        add_pair_body,
        scal,
        [keep, got],
        [whole((256, n))] * 2,
        [sds((128, n))] * 2,
        [whole((128, n))] * 2,
    )


def add_swapped_body(s, mine, got, out):
    for p in range(4):
        a, b = p * 128, (p ^ 1) * 128
        out[a : a + 128] = (
            mine[a : a + 128].astype(F32) + got[b : b + 128].astype(F32)
        ).astype(BF)


def add_swapped(scal, mine, got):
    return call(
        add_swapped_body,
        scal,
        [mine, got],
        [whole(mine.shape)] * 2,
        [sds(mine.shape)],
        [whole(mine.shape)],
    )[0]


def softmax(q, k, bias):
    z = dot_nt(q, k) * SCALE + bias
    e = jnp.exp(z - jnp.max(z, axis=1, keepdims=True))
    return e * (1.0 / jnp.sum(e, axis=1, keepdims=True))


def fwd_body(s, qa, qb, kva, kvb, cos, sin, bias, queries, keys, values, mixed):
    for p in range(4):
        a, b = p * 128, (p ^ 2) * 128
        t = kva[a : a + 128].astype(F32) + kvb[b : b + 128].astype(F32)
        keys[a : a + 128] = rotate(t[:, :128], cos[a : a + 128], sin[a : a + 128]).astype(BF)
        values[a : a + 128] = t[:, 128:].astype(BF)
    for h in range(8):
        at = slice(h * 128, h * 128 + 128)
        q = qa[:, at].astype(F32) + qb[:, at].astype(F32)
        q = rotate(q, cos[384:], sin[384:]).astype(BF)
        queries[:, at] = q
        p = softmax(q, keys[...], bias[...])
        mixed[:, at] = dot(p.astype(BF), values[...]).astype(BF)


def attention(scal, qa, qb, kva, kvb, cos, sin, bias):
    args = [qa, qb, kva, kvb, cos, sin, bias]
    outs = [sds((128, 1024)), sds((512, 128)), sds((512, 128)), sds((128, 1024))]
    return call(
        fwd_body,
        scal,
        args,
        [whole(a.shape) for a in args],
        outs,
        [whole(o.shape) for o in outs],
        flops=4 * 128 * 512 * 1024,
    )


def bwd_body(s, queries, keys, values, ga, gb, cos, sin, bias, dq, dkv, ds_all, p_all, q_all, g_all):
    cq, sq = cos[384:], -sin[384:]
    for h in range(8):
        at = slice(h * 128, h * 128 + 128)
        q = queries[:, at]
        g = (ga[:, at].astype(F32) + gb[:, at].astype(F32)).astype(BF)
        p = softmax(q, keys[...], bias[...])
        dp = dot_nt(g, values[...])
        ds = p * (dp - jnp.sum(p * dp, axis=1, keepdims=True)) * SCALE
        ds = ds.astype(BF)
        dq[:, at] = rotate(dot(ds, keys[...]), cq, sq).astype(BF)
        ds_all[at, :] = ds
        p_all[at, :] = p.astype(BF)
        q_all[at, :] = q
        g_all[at, :] = g
    dkv[:, :128] = dot_tn(ds_all[...], q_all[...]).astype(BF)
    dkv[:, 128:] = dot_tn(p_all[...], g_all[...]).astype(BF)


def attention_back(scal, queries, keys, values, ga, gb, cos, sin, bias):
    args = [queries, keys, values, ga, gb, cos, sin, bias]
    outs = [sds((128, 1024)), sds((512, 256))]
    return call(
        bwd_body,
        scal,
        args,
        [whole(a.shape) for a in args],
        outs,
        [whole(o.shape) for o in outs],
        scratch=[pltpu.VMEM((1024, 512), BF)] * 2 + [pltpu.VMEM((1024, 128), BF)] * 2,
        flops=10 * 128 * 512 * 1024,
    )


def dkv_body(s, mine, got, cos, sin, out):
    for p in range(4):
        a, b = p * 128, (p ^ 2) * 128
        t = mine[a : a + 128].astype(F32) + got[b : b + 128].astype(F32)
        out[a : a + 128, :128] = rotate(t[:, :128], cos[a : a + 128], -sin[a : a + 128]).astype(BF)
        out[a : a + 128, 128:] = t[:, 128:].astype(BF)


def dkv_final(scal, mine, got, cos, sin):
    args = [mine, got, cos, sin]
    return call(
        dkv_body,
        scal,
        args,
        [whole(a.shape) for a in args],
        [sds((512, 256))],
        [whole((512, 256))],
    )[0]


def ring_outs(rows, n):
    half = rows // 2
    return [sds((half, n))] * 2 + [sds((rows, n))] * 3


def store_ring(r, rows, outs):
    first, second, right, left, own = outs
    half = rows // 2
    own[...] = r[:rows].astype(BF)
    left[...] = r[rows : 2 * rows].astype(BF)
    right[...] = r[2 * rows : 3 * rows].astype(BF)
    first[...] = r[3 * rows : 3 * rows + half].astype(BF)
    second[...] = r[3 * rows + half :].astype(BF)


def fill_col_pieces(ref, pieces, c, base=0):
    for p, piece in enumerate(pieces):
        ref[rows_at(base + (3 ^ c ^ p)), : piece.shape[1]] = piece


def out_body(s, m0, m1, m2, m3, wo, o0, o1, o2, o3, o4, ms):
    @pl.when(pl.program_id(0) == 0)
    def _():
        fill_col_pieces(ms, [m[...] for m in (m0, m1, m2, m3)], s[0])

    store_ring(dot(ms[...], wo[...]), 128, (o0, o1, o2, o3, o4))


def out_parts(scal, mixed, wo):
    nq, feat = wo.shape
    tile = 512
    outs = ring_outs(128, feat)
    return call(
        out_body,
        scal,
        [*mixed, wo],
        [whole(m.shape) for m in mixed] + [pl.BlockSpec((nq, tile), lambda i, *_: (0, i))],
        outs,
        [pl.BlockSpec((o.shape[0], tile), lambda i, *_: (0, i)) for o in outs],
        grid=(feat // tile,),
        scratch=[pltpu.VMEM((512, nq), BF)],
        flops=2 * 512 * feat * nq,
    )


def gin_body(s, g0, g1, g2, g3, dkv, wq, wk, wv, o0, o1, o2, o3, o4, gs):
    @pl.when(pl.program_id(0) == 0)
    def _():
        fill_col_pieces(gs, [g[...] for g in (g0, g1, g2, g3)], s[0])
        for p in range(4):
            gs[rows_at(3 ^ s[0] ^ p), 1024:] = dkv[p * 128 : p * 128 + 128]

    w = jnp.concatenate([wq[...], wk[...], wv[...]], axis=1)
    store_ring(dot_nt(gs[...], w), 128, (o0, o1, o2, o3, o4))


def gin_parts(scal, dq, dkv, wq, wk, wv):
    feat, nq = wq.shape
    tile = 512
    outs = ring_outs(128, feat)
    return call(
        gin_body,
        scal,
        [*dq, dkv, wq, wk, wv],
        [whole(m.shape) for m in dq]
        + [whole(dkv.shape)]
        + [pl.BlockSpec((tile, w.shape[1]), lambda i, *_: (i, 0)) for w in (wq, wk, wv)],
        outs,
        [pl.BlockSpec((o.shape[0], tile), lambda i, *_: (0, i)) for o in outs],
        grid=(feat // tile,),
        scratch=[pltpu.VMEM((512, nq + 256), BF)],
        flops=2 * 512 * feat * (nq + 256),
    )


def wo_body(s, *refs):
    m, dy, outs, (ms, dys) = refs[:8], refs[8:18], refs[18:23], refs[23:]
    c, xx = s[0], s[3]
    fill_row_pieces(dys, [r[...] for r in dy[:5]], lambda j: j)
    fill_row_pieces(dys, [r[...] for r in dy[5:]], lambda j: j, 4)
    for j in (3, 2, 1, 0):
        at = pl.multiple_of((xx + OFFSETS[j]) % 4 * 128, 128)
        for k in range(8):
            rows = rows_at(k // 4 * 4 + (3 ^ c ^ (k % 4)))
            ms[rows, :128] = m[k][:, pl.ds(at, 128)]
            ms[rows, 128:] = m[k][:, pl.ds(at + 512, 128)]
        store_one(dot_tn(ms[...], dys[...]), j, outs)


def store_one(r, j, outs):
    first, second, right, left, own = outs
    r = r.astype(BF)
    if j == 3:
        half = r.shape[0] // 2
        first[...] = r[:half]
        second[...] = r[half:]
    else:
        (own, left, right)[j][...] = r


def wo_parts(scal, mixed, mixed_other, dy, dy_other):
    outs = ring_outs(256, 1024)
    return call(
        wo_body,
        scal,
        [*mixed, *mixed_other, *dy, *dy_other],
        [whole((128, 1024))] * 8
        + [pl.BlockSpec((p.shape[0], 1024), lambda i, s: (0, s[2])) for p in dy]
        + [pl.BlockSpec((p.shape[0], 1024), lambda i, s: (0, 0)) for p in dy_other],
        outs,
        [whole(o.shape) for o in outs],
        scratch=[pltpu.VMEM((1024, 256), BF), pltpu.VMEM((1024, 1024), BF)],
        flops=2 * 1024 * 1024 * 1024,
        limit=32,
    )


def w_body(s, *refs):
    g, dkv, x, outs, (xs, gs) = refs[:8], refs[8:10], refs[10:20], refs[20:25], refs[25:]
    c, xx = s[0], s[3]
    for k in range(8):
        rows = rows_at(k // 4 * 4 + (3 ^ c ^ (k % 4)))
        p = k % 4 * 128
        gs[rows, :1024] = g[k][...]
        gs[rows, 1024:] = dkv[k // 4][p : p + 128]
    for j in (3, 2, 1, 0):
        at = pl.ds(pl.multiple_of((xx + OFFSETS[j]) % 4 * 256, 256), 256)
        fill_row_pieces(xs, [r[:, at] for r in x[:5]], lambda j: j)
        fill_row_pieces(xs, [r[:, at] for r in x[5:]], lambda j: j, 4)
        store_one(dot_tn(xs[...], gs[...]), j, outs)


def w_parts(scal, dq, dq_other, dkv, dkv_other, x, x_other):
    outs = ring_outs(256, 1280)
    return call(
        w_body,
        scal,
        [*dq, *dq_other, dkv, dkv_other, *x, *x_other],
        [whole((128, 1024))] * 8
        + [whole((512, 256))] * 2
        + [pl.BlockSpec((p.shape[0], 1024), lambda i, s: (0, s[2])) for p in x]
        + [pl.BlockSpec((p.shape[0], 1024), lambda i, s: (0, 1)) for p in x_other],
        outs,
        [whole(o.shape) for o in outs],
        scratch=[pltpu.VMEM((1024, 256), BF), pltpu.VMEM((1024, 1280), BF)],
        flops=2 * 1024 * 1024 * 1280,
        limit=32,
    )


def ring_add_body(s, right, left, first, second, right_out, left_out):
    half = first.shape[0]
    right_out[:half] = (right[:half].astype(F32) + first[...].astype(F32)).astype(BF)
    right_out[half:] = right[half:]
    left_out[:half] = left[:half]
    left_out[half:] = (left[half:].astype(F32) + second[...].astype(F32)).astype(BF)


def ring_sum(scal, parts, shift):
    first, second, right, left, own = parts
    args = [right, left, shift(first, 1), shift(second, -1)]
    right, left = call(
        ring_add_body,
        scal,
        args,
        [whole(a.shape) for a in args],
        [sds(right.shape)] * 2,
        [whole(right.shape)] * 2,
    )
    got_left = shift(right, 1)
    got_right = shift(left, -1)
    return own.astype(F32) + got_left.astype(F32) + got_right.astype(F32)


def on_device(inputs, w_query, w_key, w_value, w_output, segment_ids, position_gaps, cotangent):
    row = lax.axis_index("row")
    col = lax.axis_index("col")
    depth = lax.axis_index("depth")
    yhi, xx = depth // 4, depth % 4
    scal = jnp.stack([col, row, yhi, xx]).astype(jnp.int32)
    x_own, dy_own = inputs[0], cotangent[0]
    half_feat = x_own.shape[1] // 2

    def half(v, which):
        return lax.dynamic_slice_in_dim(v, which * half_feat, half_feat, 1)

    both_own = swap_yhi(jnp.concatenate([half(dy_own, 1 - yhi), half(x_own, 1 - yhi)], axis=1))

    blocks = jnp.array(OFFSETS, jnp.int32)[col ^ (3 - jnp.arange(4, dtype=jnp.int32))]
    blocks = (row + blocks) % 4
    token = (blocks[:, None] * 128 + jnp.arange(128, dtype=jnp.int32)).reshape(512)
    segments = segment_ids[0]
    gaps = position_gaps[0].astype(F32)
    seg = jnp.take(segments.reshape(4, 128), blocks, axis=0).reshape(512)
    natural = jnp.arange(512, dtype=jnp.int32)
    earlier = (seg[:, None] == segments[None, :]) & (natural[None, :] < token[:, None])
    positions = jnp.sum(jnp.where(earlier, gaps[None, :], 0.0), axis=1)
    frequency = 1.0 / 10000.0 ** (jnp.arange(64, dtype=F32) * (2.0 / HEAD))
    angles = positions[:, None] * frequency[None, :]
    cos, sin = jnp.cos(angles), jnp.sin(angles)
    cos = jnp.concatenate([cos, cos], axis=1)
    sin = jnp.concatenate([-sin, sin], axis=1)
    allowed = (seg[384:, None] == seg[None, :]) & (token[None, :] <= token[384:, None])
    bias = jnp.where(allowed, 0.0, -jnp.inf).astype(F32)

    x = gather_row(x_own)
    dy = gather_row(after(dy_own, x[3], x[4]))
    both = gather_row(after(both_own, dy[3], dy[4]))

    kv, q_send, q_keep = qkv_parts(scal, x, w_query, w_key, w_value)
    kv = add_swapped(scal, kv, swap_core(kv))
    kv_got = swap_ylo(kv)
    q_send, q_keep = add_pair(scal, q_keep, swap_core(q_send))
    q_got = swap_ylo(q_send)
    queries, keys, values, mixed_own = attention(scal, q_keep, q_got, kv, kv_got, cos, sin, bias)

    def gather_y(v):
        a = swap_ylo(v)
        o = swap_yhi(v)
        b = swap_other(v)
        return [swap_core(a), a, swap_core(v), v], [swap_core(b), b, swap_core(o), o]

    mixed, mixed_other = gather_y(mixed_own)

    g_send, g_keep = gm_parts(scal, dy, w_output)
    g_send, g_keep = add_pair(scal, g_keep, swap_core(g_send))
    g_got = swap_ylo(g_send)

    attn_out = ring_sum(scal, out_parts(scal, mixed, w_output), shift_row)

    dq_own, dkv = attention_back(
        scal, queries, keys, values, g_keep, g_got, cos, sin, bias
    )
    dkv = add_swapped(scal, dkv, swap_core(dkv))
    dkv = dkv_final(scal, dkv, swap_ylo(dkv), cos, sin)
    dkv_other = swap_yhi(dkv)
    dq, dq_other = gather_y(dq_own)

    wo_sum = ring_sum(scal, wo_parts(scal, mixed, mixed_other, dy, both), shift_x)
    wo_keep = lax.dynamic_slice_in_dim(wo_sum, yhi * 128, 128, 0)
    wo_send = lax.dynamic_slice_in_dim(wo_sum, (1 - yhi) * 128, 128, 0).astype(BF)
    wo_got = swap_yhi(wo_send).astype(F32)
    grad_wo = jnp.where(
        yhi == 0,
        jnp.concatenate([wo_keep, wo_got], axis=1),
        jnp.concatenate([wo_got, wo_keep], axis=1),
    )

    grad_inputs = ring_sum(
        scal, gin_parts(scal, dq, dkv, w_query, w_key, w_value), shift_row
    )
    grad_w = ring_sum(scal, w_parts(scal, dq, dq_other, dkv, dkv_other, x, both), shift_x)
    return (
        attn_out.astype(BF)[None],
        grad_inputs.astype(BF)[None],
        grad_w[:, :1024],
        grad_w[:, 1024:1152],
        grad_w[:, 1152:],
        grad_wo,
    )


def solution(mesh):
    return jax.shard_map(
        on_device,
        mesh=mesh,
        in_specs=(
            P("depth", "row", "col"),
            P("col", "row"),
            P("col", "row"),
            P("col", "row"),
            P("row", "col"),
            P("depth", None),
            P("depth", None),
            P("depth", "row", "col"),
        ),
        out_specs=(
            P("depth", "row", "col"),
            P("depth", "row", "col"),
            P(("col", "depth"), "row"),
            P(("col", "depth"), "row"),
            P(("col", "depth"), "row"),
            P(("row", "depth"), "col"),
        ),
        check_vma=False,
    )
```

```python
import math

import jax
import jax.numpy as jnp
from jax import lax
from jax.experimental import pallas as pl
from jax.experimental.pallas import tpu as pltpu
from jax.sharding import PartitionSpec as P

HEAD = 128
OFFSETS = (0, 3, 1, 2)
BF = jnp.bfloat16
F32 = jnp.float32
SCALE = 1.0 / math.sqrt(HEAD)
MIB = 1 << 20
BIG = 56


def shift_row(v, s):
    return lax.ppermute(v, "row", [(i, (i + s) % 4) for i in range(4)])


def shift_x(v, s):
    return lax.ppermute(
        v, "depth", [(h * 4 + i, h * 4 + (i + s) % 4) for h in range(2) for i in range(4)]
    )


def swap_core(v):
    return lax.ppermute(v, "col", [(i, i ^ 1) for i in range(4)])


def swap_ylo(v):
    return lax.ppermute(v, "col", [(i, i ^ 2) for i in range(4)])


def swap_yhi(v):
    return lax.ppermute(v, "depth", [(i, i ^ 4) for i in range(8)])


def swap_other(v):
    pairs = [(c * 8 + d, (c ^ 2) * 8 + (d ^ 4)) for c in range(4) for d in range(8)]
    return lax.ppermute(v, ("col", "depth"), pairs)


def after(v, *deps):
    return lax.optimization_barrier((v,) + deps)[0]


def gather_row(v):
    half = v.shape[0] // 2
    left = shift_row(v, 1)
    right = shift_row(v, -1)
    return [v, left, right, shift_row(left[:half], 1), shift_row(right[half:], -1)]


def rows_at(block, size=128):
    return pl.ds(pl.multiple_of(block * size, size), size)


class Copies:
    def __init__(self, sems):
        self.sems, self.used = sems, 0

    def start(self, src, dst):
        copy = pltpu.make_async_copy(src, dst, self.sems.at[self.used])
        self.used += 1
        copy.start()
        return copy

    def row_pieces(self, pieces, ref, place, lanes=None):
        opp = place(3) * 2
        rows = [rows_at(place(j)) for j in range(3)] + [rows_at(opp, 64), rows_at(opp + 1, 64)]
        return [
            self.start(piece if lanes is None else piece.at[:, lanes], ref.at[at])
            for piece, at in zip(pieces, rows)
        ]


def wait_all(copies):
    for copy in copies:
        copy.wait()


HBM = pl.BlockSpec(memory_space=pltpu.HBM)


def dot(a, b):
    return jnp.dot(a, b, preferred_element_type=F32)


def dot_nt(a, b):
    return lax.dot_general(a, b, (((1,), (1,)), ((), ())), preferred_element_type=F32)


def dot_tn(a, b):
    return lax.dot_general(a, b, (((0,), (0,)), ((), ())), preferred_element_type=F32)


def rotate(v, cos, sin):
    return v * cos + pltpu.roll(v, 64, 1) * sin


def whole(shape):
    return pl.BlockSpec(shape, lambda *_: (0,) * len(shape))


def sds(shape, dtype=BF):
    return jax.ShapeDtypeStruct(shape, dtype)


def call(body, scal, args, in_specs, outs, out_specs, grid=(1,), scratch=(), flops=0, limit=14):
    moved = sum(a.size * a.dtype.itemsize for a in args)
    return pl.pallas_call(
        body,
        grid_spec=pltpu.PrefetchScalarGridSpec(
            num_scalar_prefetch=1,
            grid=grid,
            in_specs=in_specs,
            out_specs=out_specs,
            scratch_shapes=list(scratch),
        ),
        out_shape=outs,
        compiler_params=pltpu.CompilerParams(vmem_limit_bytes=limit * MIB),
        cost_estimate=pl.CostEstimate(flops=flops, bytes_accessed=moved, transcendentals=0),
    )(scal, *args)


def qkv_body(s, *refs):
    x, (wq, wk, wv, send, keep, xs, w, sems) = refs[:5], refs[5:]
    c = s[0]
    copies = Copies(sems)
    nq = wq.shape[1]
    xc = copies.row_pieces(x, xs, lambda j: 3 ^ c ^ j)
    kvc = [
        copies.start(wk, w.at[:, nq : nq + 128]),
        copies.start(wv, w.at[:, nq + 128 : nq + 256]),
    ]
    tiles = [slice(a, a + 256) for a in range(0, nq, 256)]
    qc = [copies.start(wq.at[:, at], w.at[:, at]) for at in tiles]
    wait_all(xc + kvc)
    r = dot(xs[...], w[:, nq:]).astype(BF)
    for p in range(4):
        send[256:, p * 256 : p * 256 + 256] = r[p * 128 : p * 128 + 128]
    for at, copy in zip(tiles, qc):
        copy.wait()
        r = dot(xs[...], w[:, at]).astype(BF)
        store_pair(r, send.at[:, at], keep.at[:, at])


def qkv_parts(scal, x, wq, wk, wv):
    feat, nq = wq.shape
    return call(
        qkv_body,
        scal,
        [*x, wq, wk, wv],
        [HBM] * 8,
        [sds((384, nq)), sds((256, nq))],
        [whole((384, nq)), whole((256, nq))],
        scratch=[
            pltpu.VMEM((512, feat), BF),
            pltpu.VMEM((feat, nq + 256), BF),
            pltpu.SemaphoreType.DMA((11,)),
        ],
        limit=BIG,
        flops=2 * 512 * feat * (nq + 256),
    )


def store_pair(r, send, keep):
    send[:128] = r[:128]
    send[128:256] = r[256:384]
    keep[:128] = r[128:256]
    keep[128:] = r[384:]


def fill_row_pieces(ref, pieces, place):
    for j in range(3):
        ref[rows_at(place(j)), :] = pieces[j][...]
    opp = place(3) * 2
    ref[rows_at(opp, 64), :] = pieces[3][...]
    ref[rows_at(opp + 1, 64), :] = pieces[4][...]


def gm_body(s, *refs):
    dy, (wo, send, keep, xs) = refs[:5], refs[5:]
    c = s[0]

    @pl.when(pl.program_id(0) == 0)
    def _():
        fill_row_pieces(xs, dy, lambda j: 3 ^ c ^ j)

    r = dot_nt(xs[...], wo[...]).astype(BF)
    store_pair(r, send, keep)


def gm_parts(scal, dy, wo):
    nq, feat = wo.shape
    tile = 256
    return call(
        gm_body,
        scal,
        [*dy, wo],
        [whole(p.shape) for p in dy] + [pl.BlockSpec((tile, feat), lambda i, *_: (i, 0))],
        [sds((256, nq)), sds((256, nq))],
        [pl.BlockSpec((256, tile), lambda i, *_: (0, i))] * 2,
        grid=(nq // tile,),
        scratch=[pltpu.VMEM((512, feat), BF)],
        flops=2 * 512 * feat * nq,
    )


def add_pair_body(s, keep, got, send, left):
    t = keep[...].astype(F32) + got[...].astype(F32)
    send[...] = t[:128].astype(BF)
    left[...] = t[128:].astype(BF)


def add_pair(scal, keep, got):
    n = keep.shape[1]
    return call(
        add_pair_body,
        scal,
        [keep, got],
        [whole((256, n))] * 2,
        [sds((128, n))] * 2,
        [whole((128, n))] * 2,
    )


def add_qkv_body(s, keep, mine, got, send, left):
    t = keep[...].astype(F32) + got[:256].astype(F32)
    send[:128] = t[:128].astype(BF)
    left[...] = t[128:].astype(BF)
    for p in range(4):
        a, b = p * 256, (p ^ 1) * 256
        send[128:, a : a + 256] = (
            mine[256:, a : a + 256].astype(F32) + got[256:, b : b + 256].astype(F32)
        ).astype(BF)


def add_qkv(scal, keep, mine, got):
    n = keep.shape[1]
    return call(
        add_qkv_body,
        scal,
        [keep, mine, got],
        [whole(keep.shape), whole(mine.shape), whole(got.shape)],
        [sds((256, n)), sds((128, n))],
        [whole((256, n)), whole((128, n))],
    )


def softmax(q, k, bias):
    z = dot_nt(q, k) * SCALE + bias
    e = jnp.exp(z - jnp.max(z, axis=1, keepdims=True))
    return e * (1.0 / jnp.sum(e, axis=1, keepdims=True))


def fwd_body(s, qa, kva, got, cos, sin, bias, queries, keys, values, mixed):
    for p in range(4):
        a, b = p * 256, (p ^ 2) * 256
        at = slice(p * 128, p * 128 + 128)
        t = kva[128:, a : a + 256].astype(F32) + got[128:, b : b + 256].astype(F32)
        keys[at] = rotate(t[:, :128], cos[at], sin[at]).astype(BF)
        values[at] = t[:, 128:].astype(BF)
    for h in range(8):
        at = slice(h * 128, h * 128 + 128)
        q = qa[:, at].astype(F32) + got[:128, at].astype(F32)
        q = rotate(q, cos[384:], sin[384:]).astype(BF)
        queries[:, at] = q
        p = softmax(q, keys[...], bias[...])
        mixed[:, at] = dot(p.astype(BF), values[...]).astype(BF)


def attention(scal, qa, kva, got, cos, sin, bias):
    args = [qa, kva, got, cos, sin, bias]
    outs = [sds((128, 1024)), sds((512, 128)), sds((512, 128)), sds((128, 1024))]
    return call(
        fwd_body,
        scal,
        args,
        [whole(a.shape) for a in args],
        outs,
        [whole(o.shape) for o in outs],
        flops=4 * 128 * 512 * 1024,
    )


def bwd_body(s, queries, keys, values, ga, gb, cos, sin, bias, out, ds_all, p_all, q_all, g_all):
    for h in range(8):
        at = slice(h * 128, h * 128 + 128)
        q = queries[:, at]
        g = (ga[:, at].astype(F32) + gb[:, at].astype(F32)).astype(BF)
        p = softmax(q, keys[...], bias[...])
        dp = dot_nt(g, values[...])
        ds = p * (dp - jnp.sum(p * dp, axis=1, keepdims=True)) * SCALE
        ds = ds.astype(BF)
        out[:128, at] = rotate(dot(ds, keys[...]), cos[384:], -sin[384:]).astype(BF)
        ds_all[at, :] = ds
        p_all[at, :] = p.astype(BF)
        q_all[at, :] = q
        g_all[at, :] = g
    dk = dot_tn(ds_all[...], q_all[...])
    dv = dot_tn(p_all[...], g_all[...])
    for p in range(4):
        at = slice(p * 128, p * 128 + 128)
        a = p * 256
        out[128:, a : a + 128] = rotate(dk[at], cos[at], -sin[at]).astype(BF)
        out[128:, a + 128 : a + 256] = dv[at].astype(BF)


def attention_back(scal, queries, keys, values, ga, gb, cos, sin, bias):
    args = [queries, keys, values, ga, gb, cos, sin, bias]
    return call(
        bwd_body,
        scal,
        args,
        [whole(a.shape) for a in args],
        [sds((256, 1024))],
        [whole((256, 1024))],
        scratch=[pltpu.VMEM((1024, 512), BF)] * 2 + [pltpu.VMEM((1024, 128), BF)] * 2,
        flops=10 * 128 * 512 * 1024,
    )[0]


def fill_grad_pieces(ref, pieces, place):
    for k in range(4):
        ref[rows_at(place(k)), :1024] = pieces[k, :128]
    for p in range(4):
        t = 0.0
        for k in range(4):
            a = (p ^ 3 ^ k) * 256
            t = t + pieces[k, 128:, a : a + 256].astype(F32)
        ref[rows_at(place(p)), 1024:] = t.astype(BF)


def ring_outs(rows, n):
    half = rows // 2
    return [sds((half, n))] * 2 + [sds((rows, n))] * 3


def store_ring(r, rows, outs, at):
    first, second, right, left, own = outs
    half = rows // 2
    own[:, at] = r[:rows].astype(BF)
    left[:, at] = r[rows : 2 * rows].astype(BF)
    right[:, at] = r[2 * rows : 3 * rows].astype(BF)
    first[:, at] = r[3 * rows : 3 * rows + half].astype(BF)
    second[:, at] = r[3 * rows + half :].astype(BF)


def out_body(s, *refs):
    m, wo, outs, (ms, w, sems) = refs[:4], refs[4], refs[5:10], refs[10:]
    c = s[0]
    copies = Copies(sems)
    mc = [copies.start(m[p], ms.at[rows_at(3 ^ c ^ p)]) for p in range(4)]
    tiles = [slice(a, a + 512) for a in range(0, wo.shape[1], 512)]
    wc = [copies.start(wo.at[:, at], w.at[:, at]) for at in tiles]
    wait_all(mc)
    for at, copy in zip(tiles, wc):
        copy.wait()
        store_ring(dot(ms[...], w[:, at]), 128, outs, at)


def out_parts(scal, mixed, wo):
    nq, feat = wo.shape
    outs = ring_outs(128, feat)
    return call(
        out_body,
        scal,
        [*mixed, wo],
        [HBM] * 5,
        outs,
        [whole(o.shape) for o in outs],
        scratch=[
            pltpu.VMEM((512, nq), BF),
            pltpu.VMEM((nq, feat), BF),
            pltpu.SemaphoreType.DMA((8,)),
        ],
        limit=BIG,
        flops=2 * 512 * feat * nq,
    )


def gin_body(s, *refs):
    g, (wq, wk, wv), outs, (gp, gs, w, sems) = refs[:4], refs[4:7], refs[7:12], refs[12:]
    c = s[0]
    copies = Copies(sems)
    gc = [copies.start(g[k], gp.at[k]) for k in range(4)]
    feat, nq = wq.shape
    tiles = [slice(a, a + 512) for a in range(0, feat, 512)]
    wc = [
        [
            copies.start(wq.at[at], w.at[at, :nq]),
            copies.start(wk.at[at], w.at[at, nq : nq + 128]),
            copies.start(wv.at[at], w.at[at, nq + 128 :]),
        ]
        for at in tiles
    ]
    wait_all(gc)
    fill_grad_pieces(gs, gp, lambda p: 3 ^ c ^ p)
    for at, cs in zip(tiles, wc):
        wait_all(cs)
        store_ring(dot_nt(gs[...], w[at]), 128, outs, at)


def gin_parts(scal, dq, wq, wk, wv):
    feat, nq = wq.shape
    outs = ring_outs(128, feat)
    return call(
        gin_body,
        scal,
        [*dq, wq, wk, wv],
        [HBM] * 7,
        outs,
        [whole(o.shape) for o in outs],
        scratch=[
            pltpu.VMEM((4, 256, nq), BF),
            pltpu.VMEM((512, nq + 256), BF),
            pltpu.VMEM((feat, nq + 256), BF),
            pltpu.SemaphoreType.DMA((16,)),
        ],
        limit=BIG,
        flops=2 * 512 * feat * (nq + 256),
    )


def wo_body(s, *refs):
    m, dy, outs, (mp, ms, dys, sems) = refs[:8], refs[8:18], refs[18:23], refs[23:]
    c, xx = s[0], s[3]
    copies = Copies(sems)
    mc = []
    for k in range(8):
        mc.append(copies.start(m[k], mp.at[rows_at(k // 4 * 4 + (3 ^ c ^ (k % 4)))]))
    lanes = pl.ds(pl.multiple_of(s[2] * 1024, 1024), 1024)
    dc = copies.row_pieces(dy[:5], dys, lambda j: j, lanes)
    dc += copies.row_pieces(dy[5:], dys, lambda j: 4 + j, slice(0, 1024))
    wait_all(mc + dc)
    for j in (3, 2, 1, 0):
        at = pl.multiple_of((xx + OFFSETS[j]) % 4 * 128, 128)
        ms[:, :128] = mp[:, pl.ds(at, 128)]
        ms[:, 128:] = mp[:, pl.ds(at + 512, 128)]
        store_one(dot_tn(ms[...], dys[...]), j, outs)


def store_one(r, j, outs):
    first, second, right, left, own = outs
    r = r.astype(BF)
    if j == 3:
        half = r.shape[0] // 2
        first[...] = r[:half]
        second[...] = r[half:]
    else:
        (own, left, right)[j][...] = r


def wo_parts(scal, mixed, mixed_other, dy, dy_other):
    outs = ring_outs(256, 1024)
    return call(
        wo_body,
        scal,
        [*mixed, *mixed_other, *dy, *dy_other],
        [HBM] * 18,
        outs,
        [whole(o.shape) for o in outs],
        scratch=[
            pltpu.VMEM((1024, 1024), BF),
            pltpu.VMEM((1024, 256), BF),
            pltpu.VMEM((1024, 1024), BF),
            pltpu.SemaphoreType.DMA((18,)),
        ],
        limit=BIG,
        flops=2 * 1024 * 1024 * 1024,
    )


def w_body(s, *refs):
    g, x, outs, (gp, xs, gs, sems) = refs[:8], refs[8:18], refs[18:23], refs[23:]
    c, xx = s[0], s[3]
    copies = Copies(sems)
    gc = [copies.start(g[k], gp.at[k]) for k in range(8)]
    lanes = pl.ds(pl.multiple_of(s[2] * 1024, 1024), 1024)
    xc = copies.row_pieces(x[:5], xs, lambda j: j, lanes)
    xc += copies.row_pieces(x[5:], xs, lambda j: 4 + j, slice(1024, 2048))
    wait_all(gc)
    fill_grad_pieces(gs, gp.at[:4], lambda p: 3 ^ c ^ p)
    fill_grad_pieces(gs, gp.at[4:], lambda p: 4 + (3 ^ c ^ p))
    wait_all(xc)
    for j in (3, 2, 1, 0):
        at = pl.ds(pl.multiple_of((xx + OFFSETS[j]) % 4 * 256, 256), 256)
        store_one(dot_tn(xs[:, at], gs[...]), j, outs)


def w_parts(scal, dq, dq_other, x, x_other):
    outs = ring_outs(256, 1280)
    return call(
        w_body,
        scal,
        [*dq, *dq_other, *x, *x_other],
        [HBM] * 18,
        outs,
        [whole(o.shape) for o in outs],
        scratch=[
            pltpu.VMEM((8, 256, 1024), BF),
            pltpu.VMEM((1024, 1024), BF),
            pltpu.VMEM((1024, 1280), BF),
            pltpu.SemaphoreType.DMA((18,)),
        ],
        limit=BIG,
        flops=2 * 1024 * 1024 * 1280,
    )


def ring_add_body(s, right, left, first, second, right_out, left_out):
    half = first.shape[0]
    right_out[:half] = (right[:half].astype(F32) + first[...].astype(F32)).astype(BF)
    right_out[half:] = right[half:]
    left_out[:half] = left[:half]
    left_out[half:] = (left[half:].astype(F32) + second[...].astype(F32)).astype(BF)


def ring_sum(scal, parts, shift, then=()):
    first, second, right, left, own = parts
    right, left = after(right, *then), after(left, *then)
    args = [right, left, shift(first, 1), shift(second, -1)]
    right, left = call(
        ring_add_body,
        scal,
        args,
        [whole(a.shape) for a in args],
        [sds(right.shape)] * 2,
        [whole(right.shape)] * 2,
    )
    got_left = shift(right, 1)
    got_right = shift(left, -1)
    return own.astype(F32) + got_left.astype(F32) + got_right.astype(F32)


def on_device(inputs, w_query, w_key, w_value, w_output, segment_ids, position_gaps, cotangent):
    row = lax.axis_index("row")
    col = lax.axis_index("col")
    depth = lax.axis_index("depth")
    yhi, xx = depth // 4, depth % 4
    x_own, dy_own = inputs[0], cotangent[0]
    half_feat = x_own.shape[1] // 2

    def half(v, which):
        return lax.dynamic_slice_in_dim(v, which * half_feat, half_feat, 1)

    both_own = swap_yhi(jnp.concatenate([half(dy_own, 1 - yhi), half(x_own, 1 - yhi)], axis=1))

    blocks = jnp.array(OFFSETS, jnp.int32)[col ^ (3 - jnp.arange(4, dtype=jnp.int32))]
    blocks = (row + blocks) % 4
    scal = jnp.concatenate([jnp.stack([col, row, yhi, xx]).astype(jnp.int32), blocks])
    token = (blocks[:, None] * 128 + jnp.arange(128, dtype=jnp.int32)).reshape(512)
    segments = segment_ids[0]
    gaps = position_gaps[0].astype(F32)
    seg = jnp.take(segments.reshape(4, 128), blocks, axis=0).reshape(512)
    natural = jnp.arange(512, dtype=jnp.int32)
    earlier = (seg[:, None] == segments[None, :]) & (natural[None, :] < token[:, None])
    positions = jnp.sum(jnp.where(earlier, gaps[None, :], 0.0), axis=1)
    frequency = 1.0 / 10000.0 ** (jnp.arange(64, dtype=F32) * (2.0 / HEAD))
    angles = positions[:, None] * frequency[None, :]
    cos, sin = jnp.cos(angles), jnp.sin(angles)
    cos = jnp.concatenate([cos, cos], axis=1)
    sin = jnp.concatenate([-sin, sin], axis=1)
    allowed = (seg[384:, None] == seg[None, :]) & (token[None, :] <= token[384:, None])
    bias = jnp.where(allowed, 0.0, -jnp.inf).astype(F32)

    x = gather_row(x_own)
    dy = gather_row(after(dy_own, x[3], x[4]))
    both = gather_row(after(both_own, dy[3], dy[4]))

    send, q_keep = qkv_parts(scal, x, w_query, w_key, w_value)
    send = after(send, *dy[1:3])
    send, q_keep = add_qkv(scal, q_keep, send, swap_core(send))
    q_got = swap_ylo(send)
    g_send, g_keep = gm_parts(scal, [after(dy[0], q_got), *dy[1:]], w_output)
    queries, keys, values, mixed_own = attention(scal, q_keep, send, q_got, cos, sin, bias)
    g_send, g_keep = add_pair(scal, g_keep, swap_core(g_send))
    g_got = swap_ylo(g_send)

    a, b, o, v1 = [f(mixed_own) for f in (swap_ylo, swap_other, swap_yhi, swap_core)]
    grad_own = attention_back(scal, queries, keys, values, g_keep, g_got, cos, sin, bias)
    a = after(a, grad_own)
    mixed = [swap_core(a), a, v1, mixed_own]
    out_pieces = out_parts(scal, mixed, w_output)
    b, o = after(b, out_pieces[0]), after(o, out_pieces[0])
    mixed_other = [swap_core(b), b, swap_core(o), o]

    a, v1, b, o = [f(grad_own) for f in (swap_ylo, swap_core, swap_other, swap_yhi)]
    wo_pieces = wo_parts(scal, mixed, mixed_other, dy, both)
    wo_sum = ring_sum(scal, wo_pieces, shift_x)

    a = after(a, *wo_pieces)
    grad = [swap_core(a), a, v1, grad_own]
    gin_pieces = gin_parts(scal, grad, w_query, w_key, w_value)
    b, o = after(b, *gin_pieces), after(o, *gin_pieces)
    grad_other = [swap_core(b), b, swap_core(o), o]
    w_pieces = w_parts(scal, grad, grad_other, x, both)
    attn_out = ring_sum(scal, out_pieces, shift_row, w_pieces[:1])
    grad_inputs = ring_sum(scal, gin_pieces, shift_row, w_pieces[:1])
    grad_w = ring_sum(scal, w_pieces, shift_x)
    wo_sum = after(wo_sum, w_pieces[0])

    wo_keep = lax.dynamic_slice_in_dim(wo_sum, yhi * 128, 128, 0)
    wo_send = lax.dynamic_slice_in_dim(wo_sum, (1 - yhi) * 128, 128, 0).astype(BF)
    wo_got = swap_yhi(wo_send).astype(F32)
    grad_wo = jnp.where(
        yhi == 0,
        jnp.concatenate([wo_keep, wo_got], axis=1),
        jnp.concatenate([wo_got, wo_keep], axis=1),
    )

    return (
        attn_out.astype(BF)[None],
        grad_inputs.astype(BF)[None],
        grad_w[:, :1024],
        grad_w[:, 1024:1152],
        grad_w[:, 1152:],
        grad_wo,
    )


def solution(mesh):
    return jax.shard_map(
        on_device,
        mesh=mesh,
        in_specs=(
            P("depth", "row", "col"),
            P("col", "row"),
            P("col", "row"),
            P("col", "row"),
            P("row", "col"),
            P("depth", None),
            P("depth", None),
            P("depth", "row", "col"),
        ),
        out_specs=(
            P("depth", "row", "col"),
            P("depth", "row", "col"),
            P(("col", "depth"), "row"),
            P(("col", "depth"), "row"),
            P(("col", "depth"), "row"),
            P(("row", "depth"), "col"),
        ),
        check_vma=False,
    )
```
